128 devices in a mesh: lat: 8 (over y, core), lon: 16 (over x, z).
Axes of the slice: x: 4, y: 4, z: 4, core: 2. Of those that a mesh axis runs over, the one named last changes fastest.
Arguments:
- grid_feats: bfloat16 [65536, 474], P(('lat', 'lon')), may hold values from -6 to 6
- mesh_latent: bfloat16 [65536, 512], P(('lat', 'lon')), may hold values from -6 to 6
- embed_in: bfloat16 [474, 512], replicated, may hold values from -0.25 to 0.25
- embed_out: bfloat16 [512, 512], replicated, may hold values from -0.25 to 0.25
- enc_send: bfloat16 [512, 512], replicated, may hold values from -0.25 to 0.25
- enc_recv: bfloat16 [512, 512], replicated, may hold values from -0.25 to 0.25
- enc_edge_out: bfloat16 [512, 512], replicated, may hold values from -0.25 to 0.25
- enc_node_self: bfloat16 [512, 512], replicated, may hold values from -0.25 to 0.25
- enc_node_agg: bfloat16 [512, 512], replicated, may hold values from -0.25 to 0.25
- enc_node_out: bfloat16 [512, 512], replicated, may hold values from -0.25 to 0.25
- proc_send: bfloat16 [512, 512], replicated, may hold values from -0.25 to 0.25
- proc_recv: bfloat16 [512, 512], replicated, may hold values from -0.25 to 0.25
- proc_edge_out: bfloat16 [512, 512], replicated, may hold values from -0.25 to 0.25
- proc_node_self: bfloat16 [512, 512], replicated, may hold values from -0.25 to 0.25
- proc_node_agg: bfloat16 [512, 512], replicated, may hold values from -0.25 to 0.25
- proc_node_out: bfloat16 [512, 512], replicated, may hold values from -0.25 to 0.25
- dest_dev: int32 [65536, 2], P(('lat', 'lon')), may hold values from 0 to 127, all different within a row; in each aligned block of 512 rows (0 to 511, 512 to 1023, ...) at most 16 rows name the same one
- dest_node: int32 [65536, 2], P(('lat', 'lon')), may hold values from 0 to 511
- send_rows: int32 [128, 128, 4], P(('lat', 'lon')), may hold values from 0 to 511
- src_slot: int32 [65536, 8], P(('lat', 'lon')), may hold values from 0 to 1023
Outputs:
- mesh_out: bfloat16 [65536, 512], P(('lat', 'lon'))
The draws below stay inside these ranges and needn't reach their ends.
Inputs may be any that keep to these rules, and one draw needn't show every extreme that they name: `dest_dev`: in the rows of one device, no device is named more than 16 times and some device exactly 16 times; a row's two devices differ.
All inputs are finite; a program needn't handle non-finite values.
Results may differ from the reference program's by a relative error of at most 0.017.
Values may be sent and summed in bfloat16 or wider, within the bound.
A program may use at most 64 MiB of HBM per device.

```python
import math
import jax
import jax.numpy as jnp
import numpy as np
from jax import lax

C = 474
D = 512
GR = 512
M_DEV = 512
K = 8
CAP_M = 4
CAP_E = 16
GRID = 65536
MESH = 65536
N_LAT = 8
N_LON = 16
DEVICES = 128


def plant(drawn, stream_key, low, top_value):
    longest = drawn.shape.index(max(drawn.shape))
    spots = []
    for shift in (0, 1):
        where = [jax.random.randint(jax.random.fold_in(stream_key, axis), (), 0, length) for axis, length in enumerate(drawn.shape)]
        where[longest] = (where[longest] + shift) % drawn.shape[longest]
        spots.append(tuple(where))
    return drawn.at[spots[0]].set(low).at[spots[1]].set(top_value)


def shard_levels(stream_key, shape, cuts, smallest, high):
    level = 1.0
    for axis_at, parts in cuts:
        draws = jax.random.uniform(jax.random.fold_in(jax.random.fold_in(stream_key, 6), axis_at), (parts,), jnp.float32, smallest / len(cuts), high / len(cuts))
        level = level * jnp.repeat(jnp.exp(draws), shape[axis_at] // parts).reshape((-1,) + (1,) * (len(shape) - 1 - axis_at))
    return level


def shared_out(own_key, own, number, rows, count, top, reach, slope):
    order = jax.random.permutation(own_key, count)
    crowded, usual = shares(count, rows * top, reach, slope, True), shares(count, rows * top, reach, slope, False)
    places = jnp.arange(count)

    def named(tallies, rotation):
        used = int((tallies > 0).sum())
        fixed = max(1, used // 4)
        passed = fixed + (places - fixed + rotation * (used - fixed)) % max(1, count - fixed)
        return jnp.zeros((count,), jnp.int32).at[order[jnp.where(places < fixed, places, passed)]].set(jnp.asarray(tallies, jnp.int32))

    tallies = jnp.where(number % 4 == 0, named(crowded, number // 4), named(usual, number - number // 4 - 1))
    mixed = jax.random.permutation(jax.random.fold_in(own, 3), count)
    giver, taker = mixed[0:count // 2 * 2:2], mixed[1:count // 2 * 2:2]
    slack = jnp.minimum(tallies[giver] - 1, reach - tallies[taker]) // 2
    slack = jnp.where((giver == order[0]) | (taker == order[0]) | (tallies[taker] == 0), 0, jnp.maximum(slack, 0))
    passed = jax.random.randint(jax.random.fold_in(own, 4), (count // 2,), 0, 1 << 20) % (slack + 1)
    tallies = tallies.at[giver].add(-passed).at[taker].add(passed)
    members = jnp.searchsorted(jnp.cumsum(tallies), jnp.arange(rows * top), side="right").astype(jnp.int32)
    table = members.reshape(top, rows).T
    table = table[jax.random.permutation(jax.random.fold_in(own, 1), rows)]
    rotation = jax.random.randint(jax.random.fold_in(own, 2), (rows, 1), 0, top)
    return jnp.take_along_axis(table, (jnp.arange(top)[None, :] + rotation) % top, axis=1)


def shares(count, total, limit, slope, full):
    portions = [(1 << 20) // math.isqrt(standing ** slope) + 1 for standing in range(1, count + 1)]
    largest = limit if full else min(limit, max(-(-total // count), total * portions[0] // sum(portions)))
    least = 1 if total - largest >= count - 1 else 0
    given, spare = [largest] + [least] * (count - 1), total - largest - least * (count - 1)
    while spare > 0:
        movable = [i for i in range(1, count) if given[i] < largest] or [i for i in range(1, count) if given[i] < limit]
        mass, left = sum([portions[i] for i in movable]), spare
        for i in movable:
            extra = min(limit - given[i], max(1, left * portions[i] // mass), spare)
            given[i] = given[i] + extra
            spare = spare - extra
    return np.array(given)


def centred(stream_key, shape, deviation, reach, cuts=(), kind=jnp.bfloat16):
    array = jax.random.normal(stream_key, shape, jnp.float32) * deviation
    if len(cuts) > 0:
        array = shard_levels(stream_key, shape, cuts, -0.22, 0.18) * array
    return jnp.clip(array, min=-reach, max=reach).astype(kind)


def setup_inputs(seed: int = 0) -> dict:
    splits = jax.random.split(jax.random.key(seed), 21)
    grid_feats = centred(splits[0], (GRID, C), 1.0, 6.0, ((0, 128),))
    mesh_latent = centred(splits[1], (MESH, D), 1.0, 6.0, ((0, 128),))
    embed_in = centred(splits[2], (C, D), C ** -0.5, 0.25)
    embed_out = centred(splits[3], (D, D), D ** -0.5, 0.25)
    enc_send = centred(splits[4], (D, D), D ** -0.5, 0.25)
    enc_recv = centred(splits[5], (D, D), D ** -0.5, 0.25)
    enc_edge_out = centred(splits[6], (D, D), D ** -0.5, 0.25)
    enc_node_self = centred(splits[7], (D, D), D ** -0.5, 0.25)
    enc_node_agg = centred(splits[8], (D, D), D ** -0.5, 0.25)
    enc_node_out = centred(splits[9], (D, D), D ** -0.5, 0.25)
    proc_send = centred(splits[10], (D, D), D ** -0.5, 0.25)
    proc_recv = centred(splits[11], (D, D), D ** -0.5, 0.25)
    proc_edge_out = centred(splits[12], (D, D), D ** -0.5, 0.25)
    proc_node_self = centred(splits[13], (D, D), D ** -0.5, 0.25)
    proc_node_agg = centred(splits[14], (D, D), D ** -0.5, 0.25)
    proc_node_out = centred(splits[15], (D, D), D ** -0.5, 0.25)
    dest_dev_keys = jax.random.split(jax.random.fold_in(splits[16], 1), GRID // GR)
    dest_dev_turns = jax.random.permutation(jax.random.fold_in(splits[16], 3), GRID // GR)
    dest_dev = jax.vmap(lambda own, number: shared_out(jax.random.fold_in(splits[16], 2), own, number, GR, DEVICES, 2, CAP_E, 2))(dest_dev_keys, dest_dev_turns).reshape((GRID, 2))
    dest_node = plant(jax.random.randint(splits[17], (GRID, 2), 0, M_DEV), jax.random.fold_in(splits[17], 1), 0, M_DEV - 1).astype(jnp.int32)
    send_rows = plant(jax.random.randint(splits[18], (DEVICES, DEVICES, CAP_M), 0, M_DEV), jax.random.fold_in(splits[18], 1), 0, M_DEV - 1).astype(jnp.int32)
    src_slot = plant(jax.random.randint(splits[19], (MESH, K), 0, M_DEV + DEVICES * CAP_M), jax.random.fold_in(splits[19], 1), 0, (M_DEV + DEVICES * CAP_M) - 1).astype(jnp.int32)
    return dict(grid_feats=grid_feats, mesh_latent=mesh_latent, embed_in=embed_in, embed_out=embed_out, enc_send=enc_send, enc_recv=enc_recv, enc_edge_out=enc_edge_out, enc_node_self=enc_node_self, enc_node_agg=enc_node_agg, enc_node_out=enc_node_out, proc_send=proc_send, proc_recv=proc_recv, proc_edge_out=proc_edge_out, proc_node_self=proc_node_self, proc_node_agg=proc_node_agg, proc_node_out=proc_node_out, dest_dev=dest_dev, dest_node=dest_node, send_rows=send_rows, src_slot=src_slot)


def swish_act(values):
    return values * jax.nn.sigmoid(values)


def embed_rows(features, embed_in, embed_out):
    hidden = swish_act(jnp.dot(features, embed_in, preferred_element_type=jnp.float32)).astype(jnp.bfloat16)
    return jnp.dot(hidden, embed_out, preferred_element_type=jnp.float32).astype(jnp.bfloat16)


def node_update(latent, summed, w_self, w_agg, w_out):
    preact = jnp.dot(latent, w_self, preferred_element_type=jnp.float32) + jnp.dot(summed, w_agg, preferred_element_type=jnp.float32)
    hidden = swish_act(preact).astype(jnp.bfloat16)
    return (latent.astype(jnp.float32) + jnp.dot(hidden, w_out, preferred_element_type=jnp.float32)).astype(jnp.bfloat16)


def reference(grid_feats, mesh_latent, embed_in, embed_out, enc_send, enc_recv, enc_edge_out, enc_node_self, enc_node_agg, enc_node_out, proc_send, proc_recv, proc_edge_out, proc_node_self, proc_node_agg, proc_node_out, dest_dev, dest_node, send_rows, src_slot):
    device_count = N_LAT * N_LON
    mesh_count = M_DEV * device_count
    recv_proj = jnp.dot(mesh_latent, enc_recv, preferred_element_type=jnp.float32)
    target = (dest_dev * M_DEV + dest_node).astype(jnp.int32)

    def encode_block(summed, pieces):
        features, targets = pieces
        latent = embed_rows(features, embed_in, embed_out)
        sent = jnp.dot(latent, enc_send, preferred_element_type=jnp.float32)
        preact = sent[:, None, :] + recv_proj[targets]
        hidden = swish_act(preact).astype(jnp.bfloat16).reshape(-1, D)
        messages = jnp.dot(hidden, enc_edge_out, preferred_element_type=jnp.float32)
        summed = summed.at[targets.reshape(-1)].add(messages)
        return summed, None

    summed, _ = lax.scan(encode_block, jnp.zeros((mesh_count, D), jnp.float32),
                         (grid_feats.reshape(device_count, GR, C), target.reshape(device_count, GR, 2)))
    mesh_one = node_update(mesh_latent, summed.astype(jnp.bfloat16), enc_node_self, enc_node_agg, enc_node_out)

    owner_dev = (jnp.arange(mesh_count, dtype=jnp.int32) // M_DEV)[:, None]
    remainder = jnp.maximum(src_slot - M_DEV, 0)
    peer_dev = remainder // CAP_M
    column = remainder % CAP_M
    remote = peer_dev * M_DEV + send_rows[peer_dev, owner_dev, column]
    sender = jnp.where(src_slot < M_DEV, owner_dev * M_DEV + src_slot, remote).astype(jnp.int32)
    recv_two = jnp.dot(mesh_one, proc_recv, preferred_element_type=jnp.float32)

    def process_block(pieces):
        senders, receivers, latent = pieces
        gathered = mesh_one[senders.reshape(-1)]
        preact = jnp.dot(gathered, proc_send, preferred_element_type=jnp.float32).reshape(M_DEV, K, D) + receivers[:, None, :]
        hidden = swish_act(preact).astype(jnp.bfloat16).reshape(-1, D)
        messages = jnp.dot(hidden, proc_edge_out, preferred_element_type=jnp.float32).reshape(M_DEV, K, D)
        summed_two = jnp.sum(messages, axis=1).astype(jnp.bfloat16)
        return node_update(latent, summed_two, proc_node_self, proc_node_agg, proc_node_out)

    result = lax.map(process_block, (sender.reshape(device_count, M_DEV, K), recv_two.reshape(device_count, M_DEV, D),
                                     mesh_one.reshape(device_count, M_DEV, D)))
    return result.reshape(mesh_count, D)
```

```python
import functools

import jax
import jax.numpy as jnp
from jax import lax
from jax.experimental import pallas as pl
from jax.experimental.pallas import tpu as pltpu
from jax.sharding import PartitionSpec as P

MESH = pl.DeviceIdType.MESH
BF16 = jnp.bfloat16
F32 = jnp.float32
PEERS = 128
CAP = 16
HALO = 4
GROUP = 16
GROUPS = PEERS // GROUP
DIM = 512
CHANNELS = 474
ROWS = 512
TAIL = CHANNELS // 16 * 16
DEGREE = 8

(
    EMBED_OUT,
    ENC_SEND,
    ENC_RECV,
    ENC_EDGE_OUT,
    ENC_NODE_SELF,
    ENC_NODE_AGG,
    ENC_NODE_OUT,
    PROC_SEND,
    PROC_RECV,
    PROC_EDGE_OUT,
    PROC_NODE_SELF,
    PROC_NODE_AGG,
    PROC_NODE_OUT,
) = range(13)


def ring_distance(step):
    return min(step, 4 - step)


OFFSETS = sorted(
    (
        (dy, dc, dx, dz)
        for dy in range(4)
        for dc in range(2)
        for dx in range(4)
        for dz in range(4)
        if (dy, dc, dx, dz) != (0, 0, 0, 0)
    ),
    key=lambda o: -(ring_distance(o[0]) + ring_distance(o[2]) + ring_distance(o[3]) + 0.1 * o[1]),
)


def swish(values):
    return values * (0.5 * jnp.tanh(0.5 * values) + 0.5)


def dot(left, right):
    return jnp.dot(left, right, preferred_element_type=F32)


def dot_nt(left, right):
    return lax.dot_general(left, right, (((1,), (1,)), ((), ())), preferred_element_type=F32)


def dot_tn(left, right):
    return lax.dot_general(left, right, (((0,), (0,)), ((), ())), preferred_element_type=F32)


def iota(shape, dimension):
    return lax.broadcasted_iota(jnp.int32, shape, dimension)


def kernel(
    feats_hbm,
    latent_hbm,
    embed_in_hbm,
    *rest,
):
    weights_hbm = rest[:13]
    (dest_hbm, node_hbm, send_rows_hbm, slot_hbm, out_ref) = rest[13:18]
    (
        feats,
        aug,
        latent,
        embed_raw,
        embed_in,
        weights,
        dest,
        node,
        send_rows,
        slot,
        outgoing,
        arriving,
        halo_out,
        halo_in,
        recv_proj,
        self_part,
        fold_enc,
        fold_proc,
        spread,
        hidden_sum,
        chooser,
        pick_local,
        pick_halo,
        mesh_one,
        projected,
        receiver,
        local_part,
        load_sem,
        weight_sem,
        send_sem,
        recv_sem,
        halo_send_sem,
        halo_recv_sem,
        own_sem,
    ) = rest[18:]

    lat, lon = lax.axis_index("lat"), lax.axis_index("lon")
    me = lat * 16 + lon
    lats = {(dy, dc): ((lat // 2 + dy) % 4) * 2 + (lat + dc) % 2 for dy in range(4) for dc in range(2)}
    lons = {(dx, dz): ((lon // 4 + dx) % 4) * 4 + (lon + dz) % 4 for dx in range(4) for dz in range(4)}

    def peer(offset):
        dy, dc, dx, dz = offset
        return lats[dy, dc], lons[dx, dz]

    loads = [
        pltpu.make_async_copy(source, target, load_sem.at[i])
        for i, (source, target) in enumerate(
            (
                (dest_hbm, dest),
                (node_hbm, node),
                (feats_hbm, feats),
                (latent_hbm, latent),
                (embed_in_hbm, embed_raw),
                (send_rows_hbm, send_rows),
                (slot_hbm, slot),
            )
        )
    ]
    weight_loads = [
        pltpu.make_async_copy(source, weights.at[i], weight_sem.at[i])
        for i, source in enumerate(weights_hbm)
    ]
    for load in loads:
        load.start()

    barrier = pltpu.get_barrier_semaphore()
    for offset in OFFSETS:
        pl.semaphore_signal(barrier, inc=1, device_id=peer(offset), device_id_type=MESH)
    for load in weight_loads:
        load.start()

    loads[0].wait()
    loads[1].wait()
    dests = dest[...]
    nodes = node[...]
    owner = iota((PEERS, ROWS), 0)
    hits = [dests[k : k + 1, :] == owner for k in range(2)]
    onehot = jnp.concatenate([jnp.where(hit, 1.0, 0.0).astype(BF16) for hit in hits], axis=0)
    earlier = jnp.where(iota((ROWS, ROWS), 0) < iota((ROWS, ROWS), 1), 1.0, 0.0).astype(BF16)
    ranks = dot(onehot, earlier)
    first_count = jnp.sum(jnp.where(hits[0], 1.0, 0.0), axis=1, keepdims=True)
    start = owner.astype(F32) * CAP
    positions = [
        jnp.sum(jnp.where(hits[0], ranks[:PEERS] + start, 0.0), axis=0, keepdims=True),
        jnp.sum(jnp.where(hits[1], ranks[PEERS:] + first_count + start, 0.0), axis=0, keepdims=True),
    ]
    positions = [p.astype(jnp.int32) for p in positions]

    loads[2].wait()
    aug[0:TAIL, :] = feats[0:TAIL, :]
    meta = [dests[0:1] + 1, nodes[0:1] // 32, nodes[0:1] % 32, dests[1:2] + 1, nodes[1:2] // 32, nodes[1:2] % 32]
    left = CHANNELS - TAIL
    tail = jnp.concatenate(
        [feats[TAIL:CHANNELS, :].astype(F32), jnp.zeros((16 - left, ROWS), F32)], axis=0
    )
    tail_row = iota((16, ROWS), 0)
    for i, value in enumerate(meta):
        tail = jnp.where(tail_row == left + i, value.astype(F32), tail)
    aug[TAIL : TAIL + 16, :] = tail.astype(BF16)
    aug[TAIL + 16 :, :] = jnp.zeros((DIM - TAIL - 16, ROWS), BF16)

    def pack(block, carry):
        slots = iota((512, ROWS), 0) + block * 512
        pick = jnp.where((positions[0] == slots) | (positions[1] == slots), 1.0, 0.0).astype(BF16)
        rows = dot_nt(pick, aug[...]).astype(BF16)
        outgoing[pl.ds(block * 32, 32)] = rows.reshape(32, CAP, DIM)
        return carry

    lax.fori_loop(0, PEERS * CAP // 512, pack, 0)

    pl.semaphore_wait(barrier, PEERS - 1)
    for step, offset in enumerate(OFFSETS):
        to_lat, to_lon = peer(offset)
        pltpu.make_async_remote_copy(
            src_ref=outgoing.at[to_lat * 16 + to_lon],
            dst_ref=arriving.at[step],
            send_sem=send_sem,
            recv_sem=recv_sem.at[step // GROUP],
            device_id=(to_lat, to_lon),
            device_id_type=MESH,
        ).start()
    own = pltpu.make_async_copy(outgoing.at[me], arriving.at[PEERS - 1], own_sem)
    own.start()

    loads[4].wait()
    embed_in[0:TAIL, :] = embed_raw[0:TAIL, :]
    embed_tail = jnp.concatenate(
        [embed_raw[TAIL:CHANNELS, :].astype(F32), jnp.zeros((16 - left, DIM), F32)], axis=0
    )
    embed_in[TAIL : TAIL + 16, :] = embed_tail.astype(BF16)
    embed_in[TAIL + 16 :, :] = jnp.zeros((DIM - TAIL - 16, DIM), BF16)
    loads[3].wait()
    for load in weight_loads:
        load.wait()
    recv_proj[...] = dot(latent[...], weights[ENC_RECV]).astype(BF16)
    hidden_sum[...] = jnp.zeros((ROWS, DIM), F32)
    lane = iota((128, 2 * DIM), 0) - (CHANNELS - (DIM - 128))
    right = jnp.where(iota((128, 2 * DIM), 1) >= DIM, 3, 0)
    lane = lane - right
    spread[...] = jnp.where(
        lane == 0, 512.0, jnp.where(lane == 1, 32.0, jnp.where(lane == 2, 1.0, 0.0))
    ).astype(BF16)
    self_part[...] = dot(latent[...], weights[ENC_NODE_SELF])
    fold_enc[...] = dot(weights[ENC_EDGE_OUT], weights[ENC_NODE_AGG]).astype(BF16)
    fold_proc[...] = dot(weights[PROC_EDGE_OUT], weights[PROC_NODE_AGG]).astype(BF16)

    loads[5].wait()
    loads[6].wait()
    chosen = send_rows[0]
    chosen = jnp.concatenate([chosen // 32, chosen % 32], axis=0).astype(F32).astype(BF16)
    repeat = jnp.where(iota((PEERS * HALO, PEERS), 0) // HALO == iota((PEERS * HALO, PEERS), 1), 1.0, 0.0)
    chosen = dot_nt(repeat.astype(BF16), chosen)
    column = iota((PEERS * HALO, 2 * HALO), 1)
    chosen = jnp.where(column < HALO, chosen * 32.0, chosen)
    mine = column % HALO == iota((PEERS * HALO, 2 * HALO), 0) % HALO
    chosen = jnp.sum(jnp.where(mine, chosen, 0.0), axis=1, keepdims=True).astype(jnp.int32)
    node_lane = iota((ROWS, ROWS), 1)
    chooser[...] = jnp.where(chosen == node_lane, 1.0, 0.0).astype(BF16)

    slots = slot[...]
    slots = jnp.concatenate([slots // 32, slots % 32], axis=0).astype(F32).astype(BF16)
    identity = jnp.where(iota((ROWS, ROWS), 0) == node_lane, 1.0, 0.0).astype(BF16)
    slots = dot_nt(identity, slots)
    slots = (slots[:, :DEGREE] * 32.0 + slots[:, DEGREE:]).astype(jnp.int32)
    for k in range(DEGREE):
        wanted = slots[:, k : k + 1]
        pick_local[k] = jnp.where(wanted == node_lane, 1.0, 0.0).astype(BF16)
        pick_halo[k] = jnp.where(wanted - ROWS == node_lane, 1.0, 0.0).astype(BF16)

    def arrive(group):
        rows = arriving[pl.ds(group * GROUP, GROUP)].reshape(GROUP * CAP, DIM)
        embedded = swish(dot(rows, embed_in[...])).astype(BF16)
        grid_latent = dot(embedded, weights[EMBED_OUT]).astype(BF16)
        targets = dot(rows[:, DIM - 128 :], spread[...])
        names = (iota((GROUP * CAP, DIM), 1) + 512 * (me + 1)).astype(F32)
        pick = jnp.where((targets[:, :DIM] == names) | (targets[:, DIM:] == names), 1.0, 0.0).astype(BF16)
        preact = dot(grid_latent, weights[ENC_SEND]) + dot(pick, recv_proj[...])
        hidden = swish(preact).astype(BF16)
        hidden_sum[...] += dot_tn(pick, hidden)

    def received(group, count):
        block = arriving.at[pl.ds(group * GROUP, count)]
        pltpu.make_async_remote_copy(
            src_ref=block,
            dst_ref=block,
            send_sem=send_sem,
            recv_sem=recv_sem.at[group],
            device_id=(lat, lon),
            device_id_type=MESH,
        ).wait_recv()

    def whole_group(group, carry):
        received(group, GROUP)
        arrive(group)
        return carry

    lax.fori_loop(0, GROUPS - 1, whole_group, 0)
    own.wait()
    received(GROUPS - 1, GROUP - 1)
    arrive(GROUPS - 1)

    preact = self_part[...] + dot(hidden_sum[...].astype(BF16), fold_enc[...])
    hidden = swish(preact).astype(BF16)
    updated = (latent[...].astype(F32) + dot(hidden, weights[ENC_NODE_OUT])).astype(BF16)
    mesh_one[...] = updated
    projected[...] = dot(updated, weights[PROC_SEND]).astype(BF16)
    chosen_rows = dot(chooser[...], projected[...]).astype(BF16)
    halo_out[...] = chosen_rows.reshape(PEERS, HALO, DIM)
    for offset in OFFSETS:
        to_lat, to_lon = peer(offset)
        pltpu.make_async_remote_copy(
            src_ref=halo_out.at[to_lat * 16 + to_lon],
            dst_ref=halo_in.at[me],
            send_sem=halo_send_sem,
            recv_sem=halo_recv_sem,
            device_id=(to_lat, to_lon),
            device_id_type=MESH,
        ).start()
    own_halo = pltpu.make_async_copy(halo_out.at[me], halo_in.at[me], own_sem)
    own_halo.start()

    receiver[...] = dot(mesh_one[...], weights[PROC_RECV])

    def gather_local(k, carry):
        local_part[k] = dot(pick_local[k], projected[...]) + receiver[...]
        return carry

    lax.fori_loop(0, DEGREE, gather_local, 0)
    self_part[...] = dot(mesh_one[...], weights[PROC_NODE_SELF])

    own_halo.wait()
    halo_all = halo_in.at[pl.ds(0, PEERS - 1)]
    halo_wait = pltpu.make_async_remote_copy(
        src_ref=halo_all,
        dst_ref=halo_all,
        send_sem=halo_send_sem,
        recv_sem=halo_recv_sem,
        device_id=(lat, lon),
        device_id_type=MESH,
    )
    halo_wait.wait_recv()
    table = halo_in[...].reshape(PEERS * HALO, DIM)
    hidden_sum[...] = jnp.zeros((ROWS, DIM), F32)
    projected[...] = table

    def gather_halo(k, carry):
        hidden_sum[...] += swish(local_part[k] + dot(pick_halo[k], projected[...]))
        return carry

    lax.fori_loop(0, DEGREE, gather_halo, 0)
    preact = self_part[...] + dot(hidden_sum[...].astype(BF16), fold_proc[...])
    hidden = swish(preact).astype(BF16)
    out_ref[...] = (mesh_one[...].astype(F32) + dot(hidden, weights[PROC_NODE_OUT])).astype(BF16)

    halo_wait.wait_send()
    sent = arriving.at[pl.ds(0, PEERS - 1)]
    pltpu.make_async_remote_copy(
        src_ref=sent,
        dst_ref=sent,
        send_sem=send_sem,
        recv_sem=recv_sem.at[0],
        device_id=(lat, lon),
        device_id_type=MESH,
    ).wait_send()


def on_device(grid_feats, mesh_latent, embed_in, *rest):
    weights = rest[:13]
    dest_dev, dest_node, send_rows, src_slot = rest[13:]
    vmem = pltpu.VMEM
    square = vmem((DIM, DIM), BF16)
    scratch = [
        vmem((CHANNELS, ROWS), BF16),
        vmem((DIM, ROWS), BF16),
        square,
        vmem((CHANNELS, DIM), BF16),
        square,
        vmem((13, DIM, DIM), BF16),
        vmem((2, ROWS), jnp.int32),
        vmem((2, ROWS), jnp.int32),
        vmem((1, HALO, PEERS), jnp.int32),
        vmem((DEGREE, ROWS), jnp.int32),
        vmem((PEERS, CAP, DIM), BF16),
        vmem((PEERS, CAP, DIM), BF16),
        vmem((PEERS, HALO, DIM), BF16),
        vmem((PEERS, HALO, DIM), BF16),
        square,
        vmem((ROWS, DIM), F32),
        square,
        square,
        vmem((128, 2 * DIM), BF16),
        vmem((ROWS, DIM), F32),
        vmem((PEERS * HALO, ROWS), BF16),
        vmem((DEGREE, ROWS, ROWS), BF16),
        vmem((DEGREE, ROWS, PEERS * HALO), BF16),
        square,
        square,
        vmem((ROWS, DIM), F32),
        vmem((DEGREE, ROWS, DIM), F32),
        pltpu.SemaphoreType.DMA((7,)),
        pltpu.SemaphoreType.DMA((13,)),
        pltpu.SemaphoreType.DMA,
        pltpu.SemaphoreType.DMA((GROUPS,)),
        pltpu.SemaphoreType.DMA,
        pltpu.SemaphoreType.DMA,
        pltpu.SemaphoreType.DMA,
    ]
    return pl.pallas_call(
        kernel,
        out_shape=jax.ShapeDtypeStruct((ROWS, DIM), BF16),
        in_specs=[pl.BlockSpec(memory_space=pl.ANY)] * 20,
        out_specs=pl.BlockSpec(memory_space=pltpu.VMEM),
        scratch_shapes=scratch,
        compiler_params=pltpu.CompilerParams(
            collective_id=0, has_side_effects=True, vmem_limit_bytes=56 * 2**20
        ),
    )(
        grid_feats.T,
        mesh_latent,
        embed_in,
        *weights,
        dest_dev.T,
        dest_node.T,
        jnp.swapaxes(send_rows, 1, 2),
        src_slot.T,
    )


def solution(mesh):
    rows = P(("lat", "lon"), None)
    in_specs = (rows, rows, *([P()] * 14), rows, rows, P(("lat", "lon"), None, None), rows)
    return jax.shard_map(on_device, mesh=mesh, in_specs=in_specs, out_specs=rows, check_vma=False)
```

```python
import functools

import jax
import jax.numpy as jnp
from jax import lax
from jax.experimental import pallas as pl
from jax.experimental.pallas import tpu as pltpu
from jax.sharding import PartitionSpec as P

MESH = pl.DeviceIdType.MESH
BF16 = jnp.bfloat16
F32 = jnp.float32
PEERS = 128
CAP = 16
HALO = 4
GROUP = 16
GROUPS = PEERS // GROUP
DIM = 512
CHANNELS = 474
ROWS = 512
TAIL = CHANNELS // 16 * 16
DEGREE = 8
BLOCK = GROUP * CAP

(
    EMBED_OUT,
    ENC_SEND,
    ENC_RECV,
    ENC_EDGE_OUT,
    ENC_NODE_SELF,
    ENC_NODE_AGG,
    ENC_NODE_OUT,
    PROC_SEND,
    PROC_RECV,
    PROC_EDGE_OUT,
    PROC_NODE_SELF,
    PROC_NODE_AGG,
    PROC_NODE_OUT,
) = range(13)


def ring_distance(step):
    return min(step, 4 - step)


OFFSETS = sorted(
    (
        (dy, dc, dx, dz)
        for dy in range(4)
        for dc in range(2)
        for dx in range(4)
        for dz in range(4)
        if (dy, dc, dx, dz) != (0, 0, 0, 0)
    ),
    key=lambda o: -(ring_distance(o[0]) + ring_distance(o[2]) + ring_distance(o[3]) + 0.1 * o[1]),
)


def swish(values):
    return values * (0.5 * jnp.tanh(0.5 * values) + 0.5)


def swish_half(values):
    half = (0.5 * values).astype(BF16)
    return half * jnp.tanh(half) + half


def dot(left, right):
    return jnp.dot(left, right, preferred_element_type=F32)


def dot_nt(left, right):
    return lax.dot_general(left, right, (((1,), (1,)), ((), ())), preferred_element_type=F32)


def dot_tn(left, right):
    return lax.dot_general(left, right, (((0,), (0,)), ((), ())), preferred_element_type=F32)


def iota(shape, dimension):
    return lax.broadcasted_iota(jnp.int32, shape, dimension)


def kernel(
    feats_hbm,
    latent_hbm,
    embed_in_hbm,
    *rest,
):
    weights_hbm = rest[:13]
    (dest_hbm, node_hbm, send_rows_hbm, slot_hbm, out_ref) = rest[13:18]
    (
        feats,
        aug,
        latent,
        embed_raw,
        embed_in,
        weights,
        dest,
        node,
        send_rows,
        slot,
        outgoing,
        arriving,
        halo_out,
        halo_in,
        recv_proj,
        self_part,
        fold_enc,
        fold_proc,
        sender_part,
        names_out,
        names_in,
        pick_recv,
        pick_node,
        hidden_sum,
        chooser,
        pick_local,
        pick_halo,
        mesh_one,
        projected,
        receiver,
        local_part,
        load_sem,
        weight_sem,
        send_sem,
        recv_sem,
        halo_send_sem,
        halo_recv_sem,
        own_sem,
        names_sem,
    ) = rest[18:]

    lat, lon = lax.axis_index("lat"), lax.axis_index("lon")
    me = lat * 16 + lon
    lats = {(dy, dc): ((lat // 2 + dy) % 4) * 2 + (lat + dc) % 2 for dy in range(4) for dc in range(2)}
    lons = {(dx, dz): ((lon // 4 + dx) % 4) * 4 + (lon + dz) % 4 for dx in range(4) for dz in range(4)}

    def peer(offset):
        dy, dc, dx, dz = offset
        return lats[dy, dc], lons[dx, dz]

    loads = [
        pltpu.make_async_copy(source, target, load_sem.at[i])
        for i, (source, target) in enumerate(
            (
                (dest_hbm, dest),
                (node_hbm, node),
                (feats_hbm, feats),
                (latent_hbm, latent),
                (embed_in_hbm, embed_raw),
                (send_rows_hbm, send_rows),
                (slot_hbm, slot),
            )
        )
    ]
    weight_loads = [
        pltpu.make_async_copy(source, weights.at[i], weight_sem.at[i])
        for i, source in enumerate(weights_hbm)
    ]
    for load in loads[:5]:
        load.start()
    weight_loads[EMBED_OUT].start()
    weight_loads[ENC_SEND].start()

    barrier = pltpu.get_barrier_semaphore()
    for offset in OFFSETS:
        pl.semaphore_signal(barrier, inc=1, device_id=peer(offset), device_id_type=MESH)
    for load in weight_loads[ENC_RECV:] + loads[5:]:
        load.start()

    loads[0].wait()
    loads[1].wait()
    dests = dest[...]
    nodes = node[...]
    owner = iota((PEERS, ROWS), 0)
    hits = [dests[k : k + 1, :] == owner for k in range(2)]
    onehot = [jnp.where(hit, 1.0, 0.0).astype(BF16) for hit in hits]
    earlier = jnp.where(iota((ROWS, ROWS), 0) < iota((ROWS, ROWS), 1), 1.0, 0.0).astype(BF16)
    ranks = dot(jnp.concatenate(onehot, axis=0), earlier)
    first_count = jnp.sum(jnp.where(hits[0], 1.0, 0.0), axis=1, keepdims=True)
    ranks = [
        jnp.sum(jnp.where(hits[0], ranks[:PEERS], 0.0), axis=0, keepdims=True).astype(jnp.int32),
        jnp.sum(jnp.where(hits[1], ranks[PEERS:] + first_count, 0.0), axis=0, keepdims=True).astype(jnp.int32),
    ]
    positions = [dests[k : k + 1] * CAP + ranks[k] for k in range(2)]

    named = jnp.zeros((PEERS, PEERS), F32)
    for k in range(2):
        at_slot = ranks[k] == iota((PEERS, ROWS), 0)
        label = nodes[k : k + 1] + 1
        for part in (label // 32 * 32, label % 32):
            value = jnp.where(at_slot, part.astype(F32), 0.0).astype(BF16)
            named += dot_nt(onehot[k], value)
    names_out[...] = named.reshape(PEERS, 1, PEERS)

    left = CHANNELS - TAIL
    pad = jnp.zeros((16 - left, ROWS), F32)
    rest_pad = jnp.zeros((DIM - TAIL - 16, DIM), BF16)
    for load, raw, padded in ((loads[2], feats, aug), (loads[4], embed_raw, embed_in)):
        load.wait()
        padded[0:TAIL, :] = raw[0:TAIL, :]
        padded[TAIL : TAIL + 16, :] = jnp.concatenate([raw[TAIL:CHANNELS, :].astype(F32), pad], axis=0).astype(BF16)
        padded[TAIL + 16 :, :] = rest_pad
    embedded = swish_half(dot_tn(aug[...], embed_in[...]))
    weight_loads[EMBED_OUT].wait()
    grid_latent = dot(embedded, weights[EMBED_OUT]).astype(BF16)
    weight_loads[ENC_SEND].wait()
    sender_part[...] = dot(grid_latent, weights[ENC_SEND]).astype(BF16)

    def pack(block, carry):
        slots = iota((512, ROWS), 0) + block * 512
        pick = jnp.where((positions[0] == slots) | (positions[1] == slots), 1.0, 0.0).astype(BF16)
        rows = dot(pick, sender_part[...]).astype(BF16)
        outgoing[pl.ds(block * 32, 32)] = rows.reshape(32, CAP, DIM)
        return carry

    lax.fori_loop(0, PEERS * CAP // 512, pack, 0)

    pl.semaphore_wait(barrier, PEERS - 1)
    for step, offset in enumerate(OFFSETS):
        to_lat, to_lon = peer(offset)
        pltpu.make_async_remote_copy(
            src_ref=names_out.at[to_lat * 16 + to_lon],
            dst_ref=names_in.at[step],
            send_sem=names_sem.at[0],
            recv_sem=names_sem.at[1],
            device_id=(to_lat, to_lon),
            device_id_type=MESH,
        ).start()
    own_names = pltpu.make_async_copy(names_out.at[me], names_in.at[PEERS - 1], names_sem.at[2])
    own_names.start()
    for step, offset in enumerate(OFFSETS):
        to_lat, to_lon = peer(offset)
        pltpu.make_async_remote_copy(
            src_ref=outgoing.at[to_lat * 16 + to_lon],
            dst_ref=arriving.at[step],
            send_sem=send_sem,
            recv_sem=recv_sem.at[step // GROUP],
            device_id=(to_lat, to_lon),
            device_id_type=MESH,
        ).start()
    own = pltpu.make_async_copy(outgoing.at[me], arriving.at[PEERS - 1], own_sem)
    own.start()

    loads[3].wait()
    for load in weight_loads[ENC_RECV:]:
        load.wait()
    recv_proj[...] = dot(latent[...], weights[ENC_RECV]).astype(BF16)
    hidden_sum[...] = jnp.zeros((ROWS, DIM), F32)
    self_part[...] = dot(latent[...], weights[ENC_NODE_SELF])
    fold_enc[...] = dot(weights[ENC_EDGE_OUT], weights[ENC_NODE_AGG]).astype(BF16)
    fold_proc[...] = dot(weights[PROC_EDGE_OUT], weights[PROC_NODE_AGG]).astype(BF16)

    loads[5].wait()
    loads[6].wait()
    chosen = send_rows[0]
    chosen = jnp.concatenate([chosen // 32, chosen % 32], axis=0).astype(F32).astype(BF16)
    repeat = jnp.where(iota((PEERS * HALO, PEERS), 0) // HALO == iota((PEERS * HALO, PEERS), 1), 1.0, 0.0)
    chosen = dot_nt(repeat.astype(BF16), chosen)
    column = iota((PEERS * HALO, 2 * HALO), 1)
    chosen = jnp.where(column < HALO, chosen * 32.0, chosen)
    mine = column % HALO == iota((PEERS * HALO, 2 * HALO), 0) % HALO
    chosen = jnp.sum(jnp.where(mine, chosen, 0.0), axis=1, keepdims=True).astype(jnp.int32)
    node_lane = iota((ROWS, ROWS), 1)
    chooser[...] = jnp.where(chosen == node_lane, 1.0, 0.0).astype(BF16)

    slots = slot[...]
    slots = jnp.concatenate([slots // 32, slots % 32], axis=0).astype(F32).astype(BF16)
    identity = jnp.where(iota((ROWS, ROWS), 0) == node_lane, 1.0, 0.0).astype(BF16)
    slots = dot_nt(identity, slots)
    slots = (slots[:, :DEGREE] * 32.0 + slots[:, DEGREE:]).astype(jnp.int32)
    for k in range(DEGREE):
        wanted = slots[:, k : k + 1]
        pick_local[k] = jnp.where(wanted == node_lane, 1.0, 0.0).astype(BF16)
        pick_halo[k] = jnp.where(wanted - ROWS == node_lane, 1.0, 0.0).astype(BF16)

    own_names.wait()
    names_all = names_in.at[pl.ds(0, PEERS - 1)]
    names_wait = pltpu.make_async_remote_copy(
        src_ref=names_all,
        dst_ref=names_all,
        send_sem=names_sem.at[0],
        recv_sem=names_sem.at[1],
        device_id=(lat, lon),
        device_id_type=MESH,
    )
    names_wait.wait_recv()
    labels = names_in[...].reshape(PEERS, PEERS).astype(jnp.int32)
    parts = [part.astype(F32).astype(BF16) for part in (labels // 32 * 32, labels % 32)]
    ones = jnp.ones((16, PEERS), BF16)

    def prepare(block, carry):
        first = block * BLOCK
        expand = jnp.where((iota((BLOCK, PEERS), 0) + first) // CAP == iota((BLOCK, PEERS), 1), 1.0, 0.0).astype(BF16)
        own_lane = iota((BLOCK, PEERS), 0) % CAP == iota((BLOCK, PEERS), 1)
        spread = [jnp.where(own_lane, dot(expand, part), 0.0) for part in parts]
        column = jnp.sum(spread[0] + spread[1], axis=1, keepdims=True).astype(jnp.int32) - 1
        row = (dot_nt(ones, spread[0].astype(BF16)) + dot_nt(ones, spread[1].astype(BF16)))[0:1].astype(jnp.int32) - 1
        pick = jnp.where(column == iota((BLOCK, ROWS), 1), 1.0, 0.0).astype(BF16)
        pick_recv[block] = dot(pick, recv_proj[...]).astype(BF16)
        pick_node[block] = jnp.where(row == iota((ROWS, BLOCK), 0), 1.0, 0.0).astype(BF16)
        return carry

    lax.fori_loop(0, PEERS * CAP // BLOCK, prepare, 0)

    def arrive(group):
        rows = arriving[pl.ds(group * GROUP, GROUP)].reshape(GROUP * CAP, DIM)
        hidden = swish_half(rows.astype(F32) + pick_recv[group].astype(F32))
        hidden_sum[...] += dot(pick_node[group], hidden)

    def received(group, count):
        block = arriving.at[pl.ds(group * GROUP, count)]
        pltpu.make_async_remote_copy(
            src_ref=block,
            dst_ref=block,
            send_sem=send_sem,
            recv_sem=recv_sem.at[group],
            device_id=(lat, lon),
            device_id_type=MESH,
        ).wait_recv()

    for group in range(GROUPS - 1):
        received(group, GROUP)
        arrive(group)
    own.wait()
    received(GROUPS - 1, GROUP - 1)
    arrive(GROUPS - 1)

    preact = self_part[...] + dot(hidden_sum[...].astype(BF16), fold_enc[...])
    hidden = swish(preact).astype(BF16)
    updated = (latent[...].astype(F32) + dot(hidden, weights[ENC_NODE_OUT])).astype(BF16)
    mesh_one[...] = updated
    projected[...] = dot(updated, weights[PROC_SEND]).astype(BF16)
    chosen_rows = dot(chooser[...], projected[...]).astype(BF16)
    halo_out[...] = chosen_rows.reshape(PEERS, HALO, DIM)
    for offset in OFFSETS:
        to_lat, to_lon = peer(offset)
        pltpu.make_async_remote_copy(
            src_ref=halo_out.at[to_lat * 16 + to_lon],
            dst_ref=halo_in.at[me],
            send_sem=halo_send_sem,
            recv_sem=halo_recv_sem,
            device_id=(to_lat, to_lon),
            device_id_type=MESH,
        ).start()
    own_halo = pltpu.make_async_copy(halo_out.at[me], halo_in.at[me], own_sem)
    own_halo.start()

    receiver[...] = dot(mesh_one[...], weights[PROC_RECV])

    def gather_local(k, carry):
        local_part[k] = dot(pick_local[k], projected[...]) + receiver[...]
        return carry

    lax.fori_loop(0, DEGREE, gather_local, 0)
    self_part[...] = dot(mesh_one[...], weights[PROC_NODE_SELF])

    own_halo.wait()
    halo_all = halo_in.at[pl.ds(0, PEERS - 1)]
    halo_wait = pltpu.make_async_remote_copy(
        src_ref=halo_all,
        dst_ref=halo_all,
        send_sem=halo_send_sem,
        recv_sem=halo_recv_sem,
        device_id=(lat, lon),
        device_id_type=MESH,
    )
    halo_wait.wait_recv()
    table = halo_in[...].reshape(PEERS * HALO, DIM)
    hidden_sum[...] = jnp.zeros((ROWS, DIM), F32)
    projected[...] = table

    for k in range(DEGREE):
        hidden_sum[...] += swish_half(local_part[k] + dot(pick_halo[k], projected[...])).astype(F32)

    preact = self_part[...] + dot(hidden_sum[...].astype(BF16), fold_proc[...])
    hidden = swish(preact).astype(BF16)
    out_ref[...] = (mesh_one[...].astype(F32) + dot(hidden, weights[PROC_NODE_OUT])).astype(BF16)

    names_wait.wait_send()
    halo_wait.wait_send()
    sent = arriving.at[pl.ds(0, PEERS - 1)]
    pltpu.make_async_remote_copy(
        src_ref=sent,
        dst_ref=sent,
        send_sem=send_sem,
        recv_sem=recv_sem.at[0],
        device_id=(lat, lon),
        device_id_type=MESH,
    ).wait_send()


def on_device(grid_feats, mesh_latent, embed_in, *rest):
    weights = rest[:13]
    dest_dev, dest_node, send_rows, src_slot = rest[13:]
    vmem = pltpu.VMEM
    square = vmem((DIM, DIM), BF16)
    scratch = [
        vmem((CHANNELS, ROWS), BF16),
        vmem((DIM, ROWS), BF16),
        square,
        vmem((CHANNELS, DIM), BF16),
        square,
        vmem((13, DIM, DIM), BF16),
        vmem((2, ROWS), jnp.int32),
        vmem((2, ROWS), jnp.int32),
        vmem((1, HALO, PEERS), jnp.int32),
        vmem((DEGREE, ROWS), jnp.int32),
        vmem((PEERS, CAP, DIM), BF16),
        vmem((PEERS, CAP, DIM), BF16),
        vmem((PEERS, HALO, DIM), BF16),
        vmem((PEERS, HALO, DIM), BF16),
        square,
        vmem((ROWS, DIM), F32),
        square,
        square,
        square,
        vmem((PEERS, 1, PEERS), F32),
        vmem((PEERS, 1, PEERS), F32),
        vmem((GROUPS, BLOCK, DIM), BF16),
        vmem((GROUPS, ROWS, BLOCK), BF16),
        vmem((ROWS, DIM), F32),
        vmem((PEERS * HALO, ROWS), BF16),
        vmem((DEGREE, ROWS, ROWS), BF16),
        vmem((DEGREE, ROWS, PEERS * HALO), BF16),
        square,
        square,
        vmem((ROWS, DIM), F32),
        vmem((DEGREE, ROWS, DIM), F32),
        pltpu.SemaphoreType.DMA((7,)),
        pltpu.SemaphoreType.DMA((13,)),
        pltpu.SemaphoreType.DMA,
        pltpu.SemaphoreType.DMA((GROUPS,)),
        pltpu.SemaphoreType.DMA,
        pltpu.SemaphoreType.DMA,
        pltpu.SemaphoreType.DMA,
        pltpu.SemaphoreType.DMA((3,)),
    ]
    return pl.pallas_call(
        kernel,
        out_shape=jax.ShapeDtypeStruct((ROWS, DIM), BF16),
        in_specs=[pl.BlockSpec(memory_space=pl.ANY)] * 20,
        out_specs=pl.BlockSpec(memory_space=pltpu.VMEM),
        scratch_shapes=scratch,
        compiler_params=pltpu.CompilerParams(
            collective_id=0, has_side_effects=True, vmem_limit_bytes=56 * 2**20
        ),
    )(
        grid_feats.T,
        mesh_latent,
        embed_in,
        *weights,
        dest_dev.T,
        dest_node.T,
        jnp.swapaxes(send_rows, 1, 2),
        src_slot.T,
    )


def solution(mesh):
    rows = P(("lat", "lon"), None)
    in_specs = (rows, rows, *([P()] * 14), rows, rows, P(("lat", "lon"), None, None), rows)
    return jax.shard_map(on_device, mesh=mesh, in_specs=in_specs, out_specs=rows, check_vma=False)
```

```python
import functools

import jax
import jax.numpy as jnp
from jax import lax
from jax.experimental import pallas as pl
from jax.experimental.pallas import tpu as pltpu
from jax.sharding import PartitionSpec as P

MESH = pl.DeviceIdType.MESH
BF16 = jnp.bfloat16
F32 = jnp.float32
PEERS = 128
CAP = 16
HALO = 4
GROUP = 16
GROUPS = PEERS // GROUP
DIM = 512
CHANNELS = 474
ROWS = 512
TAIL = CHANNELS // 16 * 16
DEGREE = 8
BLOCK = GROUP * CAP

(
    EMBED_OUT,
    ENC_SEND,
    ENC_RECV,
    ENC_EDGE_OUT,
    ENC_NODE_SELF,
    ENC_NODE_AGG,
    ENC_NODE_OUT,
    PROC_SEND,
    PROC_RECV,
    PROC_EDGE_OUT,
    PROC_NODE_SELF,
    PROC_NODE_AGG,
    PROC_NODE_OUT,
) = range(13)


def ring_distance(step):
    return min(step, 4 - step)


OFFSETS = sorted(
    (
        (dy, dc, dx, dz)
        for dy in range(4)
        for dc in range(2)
        for dx in range(4)
        for dz in range(4)
        if (dy, dc, dx, dz) != (0, 0, 0, 0)
    ),
    key=lambda o: -(ring_distance(o[0]) + ring_distance(o[2]) + ring_distance(o[3]) + 0.1 * o[1]),
)


def swish(values):
    return values * (0.5 * jnp.tanh(0.5 * values) + 0.5)


def swish_half(values):
    half = (0.5 * values).astype(BF16)
    return half * jnp.tanh(half) + half


def dot(left, right):
    return jnp.dot(left, right, preferred_element_type=F32)


def dot_nt(left, right):
    return lax.dot_general(left, right, (((1,), (1,)), ((), ())), preferred_element_type=F32)


def dot_tn(left, right):
    return lax.dot_general(left, right, (((0,), (0,)), ((), ())), preferred_element_type=F32)


def iota(shape, dimension):
    return lax.broadcasted_iota(jnp.int32, shape, dimension)


def kernel(
    feats_hbm,
    latent_hbm,
    embed_in_hbm,
    *rest,
):
    weights_hbm = rest[:13]
    (dest_hbm, node_hbm, send_rows_hbm, slot_hbm, out_ref) = rest[13:18]
    (
        feats,
        aug,
        latent,
        embed_raw,
        embed_in,
        weights,
        dest,
        node,
        send_rows,
        slot,
        outgoing,
        arriving,
        halo_out,
        halo_in,
        recv_proj,
        self_part,
        fold_enc,
        fold_proc,
        fold_send,
        sender_part,
        names_out,
        names_in,
        pick_recv,
        pick_node,
        hidden_sum,
        chooser,
        pick_local,
        pick_halo,
        mesh_one,
        projected,
        receiver,
        local_part,
        load_sem,
        weight_sem,
        send_sem,
        recv_sem,
        halo_send_sem,
        halo_recv_sem,
        own_sem,
        names_sem,
    ) = rest[18:]

    lat, lon = lax.axis_index("lat"), lax.axis_index("lon")
    me = lat * 16 + lon
    lats = {(dy, dc): ((lat // 2 + dy) % 4) * 2 + (lat + dc) % 2 for dy in range(4) for dc in range(2)}
    lons = {(dx, dz): ((lon // 4 + dx) % 4) * 4 + (lon + dz) % 4 for dx in range(4) for dz in range(4)}

    def peer(offset):
        dy, dc, dx, dz = offset
        return lats[dy, dc], lons[dx, dz]

    loads = [
        pltpu.make_async_copy(source, target, load_sem.at[i])
        for i, (source, target) in enumerate(
            (
                (dest_hbm, dest),
                (node_hbm, node),
                (feats_hbm, feats),
                (latent_hbm, latent),
                (embed_in_hbm, embed_raw),
                (send_rows_hbm, send_rows),
                (slot_hbm, slot),
            )
        )
    ]
    weight_loads = [
        pltpu.make_async_copy(source, weights.at[i], weight_sem.at[i])
        for i, source in enumerate(weights_hbm)
    ]
    for load in loads[:5]:
        load.start()
    weight_loads[EMBED_OUT].start()
    weight_loads[ENC_SEND].start()

    barrier = pltpu.get_barrier_semaphore()
    for offset in OFFSETS:
        pl.semaphore_signal(barrier, inc=1, device_id=peer(offset), device_id_type=MESH)
    for load in weight_loads[ENC_RECV:] + loads[5:]:
        load.start()

    loads[0].wait()
    loads[1].wait()
    dests = dest[...]
    nodes = node[...]
    owner = iota((PEERS, ROWS), 0)
    hits = [dests[k : k + 1, :] == owner for k in range(2)]
    onehot = [jnp.where(hit, 1.0, 0.0).astype(BF16) for hit in hits]
    earlier = jnp.where(iota((ROWS, ROWS), 0) < iota((ROWS, ROWS), 1), 1.0, 0.0).astype(BF16)
    ranks = dot(jnp.concatenate(onehot, axis=0), earlier)
    first_count = jnp.sum(jnp.where(hits[0], 1.0, 0.0), axis=1, keepdims=True)
    ranks = [
        jnp.sum(jnp.where(hits[0], ranks[:PEERS], 0.0), axis=0, keepdims=True).astype(jnp.int32),
        jnp.sum(jnp.where(hits[1], ranks[PEERS:] + first_count, 0.0), axis=0, keepdims=True).astype(jnp.int32),
    ]
    positions = [dests[k : k + 1] * CAP + ranks[k] for k in range(2)]

    named = jnp.zeros((PEERS, PEERS), F32)
    for k in range(2):
        at_slot = ranks[k] == iota((PEERS, ROWS), 0)
        label = nodes[k : k + 1] + 1
        for part in (label // 32 * 32, label % 32):
            value = jnp.where(at_slot, part.astype(F32), 0.0).astype(BF16)
            named += dot_nt(onehot[k], value)
    names_out[...] = named.reshape(PEERS, 1, PEERS)

    left = CHANNELS - TAIL
    pad = jnp.zeros((16 - left, ROWS), F32)
    rest_pad = jnp.zeros((DIM - TAIL - 16, DIM), BF16)
    for load, raw, padded in ((loads[2], feats, aug), (loads[4], embed_raw, embed_in)):
        load.wait()
        padded[0:TAIL, :] = raw[0:TAIL, :]
        padded[TAIL : TAIL + 16, :] = jnp.concatenate([raw[TAIL:CHANNELS, :].astype(F32), pad], axis=0).astype(BF16)
        padded[TAIL + 16 :, :] = rest_pad
    embedded = swish_half(dot_tn(aug[...], embed_in[...]))
    weight_loads[EMBED_OUT].wait()
    grid_latent = dot(embedded, weights[EMBED_OUT]).astype(BF16)
    weight_loads[ENC_SEND].wait()
    sender_part[...] = dot(grid_latent, weights[ENC_SEND]).astype(BF16)

    def pack(block, carry):
        slots = iota((512, ROWS), 0) + block * 512
        pick = jnp.where((positions[0] == slots) | (positions[1] == slots), 1.0, 0.0).astype(BF16)
        rows = dot(pick, sender_part[...]).astype(BF16)
        outgoing[pl.ds(block * 32, 32)] = rows.reshape(32, CAP, DIM)
        return carry

    lax.fori_loop(0, PEERS * CAP // 512, pack, 0)

    pl.semaphore_wait(barrier, PEERS - 1)
    for step, offset in enumerate(OFFSETS):
        to_lat, to_lon = peer(offset)
        pltpu.make_async_remote_copy(
            src_ref=names_out.at[to_lat * 16 + to_lon],
            dst_ref=names_in.at[step],
            send_sem=names_sem.at[0],
            recv_sem=names_sem.at[1],
            device_id=(to_lat, to_lon),
            device_id_type=MESH,
        ).start()
    own_names = pltpu.make_async_copy(names_out.at[me], names_in.at[PEERS - 1], names_sem.at[2])
    own_names.start()
    for step, offset in enumerate(OFFSETS):
        to_lat, to_lon = peer(offset)
        pltpu.make_async_remote_copy(
            src_ref=outgoing.at[to_lat * 16 + to_lon],
            dst_ref=arriving.at[step],
            send_sem=send_sem,
            recv_sem=recv_sem.at[step // GROUP],
            device_id=(to_lat, to_lon),
            device_id_type=MESH,
        ).start()
    own = pltpu.make_async_copy(outgoing.at[me], arriving.at[PEERS - 1], own_sem)
    own.start()

    loads[3].wait()
    for load in weight_loads[ENC_RECV:]:
        load.wait()
    recv_proj[...] = dot(latent[...], weights[ENC_RECV]).astype(BF16)
    hidden_sum[...] = jnp.zeros((ROWS, DIM), F32)
    self_part[...] = dot(latent[...], weights[ENC_NODE_SELF])
    fold_enc[...] = dot(weights[ENC_EDGE_OUT], weights[ENC_NODE_AGG]).astype(BF16)
    fold_send[...] = dot(weights[ENC_NODE_OUT], weights[PROC_SEND]).astype(BF16)
    receiver[...] = dot(latent[...], weights[PROC_SEND])
    fold_proc[...] = dot(weights[PROC_EDGE_OUT], weights[PROC_NODE_AGG]).astype(BF16)

    loads[5].wait()
    loads[6].wait()
    chosen = send_rows[0]
    chosen = jnp.concatenate([chosen // 32, chosen % 32], axis=0).astype(F32).astype(BF16)
    repeat = jnp.where(iota((PEERS * HALO, PEERS), 0) // HALO == iota((PEERS * HALO, PEERS), 1), 1.0, 0.0)
    chosen = dot_nt(repeat.astype(BF16), chosen)
    column = iota((PEERS * HALO, 2 * HALO), 1)
    chosen = jnp.where(column < HALO, chosen * 32.0, chosen)
    mine = column % HALO == iota((PEERS * HALO, 2 * HALO), 0) % HALO
    chosen = jnp.sum(jnp.where(mine, chosen, 0.0), axis=1, keepdims=True).astype(jnp.int32)
    node_lane = iota((ROWS, ROWS), 1)
    chooser[...] = jnp.where(chosen == node_lane, 1.0, 0.0).astype(BF16)

    slots = slot[...]
    slots = jnp.concatenate([slots // 32, slots % 32], axis=0).astype(F32).astype(BF16)
    identity = jnp.where(iota((ROWS, ROWS), 0) == node_lane, 1.0, 0.0).astype(BF16)
    slots = dot_nt(identity, slots)
    slots = (slots[:, :DEGREE] * 32.0 + slots[:, DEGREE:]).astype(jnp.int32)
    for k in range(DEGREE):
        wanted = slots[:, k : k + 1]
        pick_local[k] = jnp.where(wanted == node_lane, 1.0, 0.0).astype(BF16)
        pick_halo[k] = jnp.where(wanted - ROWS == node_lane, 1.0, 0.0).astype(BF16)

    own_names.wait()
    names_all = names_in.at[pl.ds(0, PEERS - 1)]
    names_wait = pltpu.make_async_remote_copy(
        src_ref=names_all,
        dst_ref=names_all,
        send_sem=names_sem.at[0],
        recv_sem=names_sem.at[1],
        device_id=(lat, lon),
        device_id_type=MESH,
    )
    names_wait.wait_recv()
    labels = names_in[...].reshape(PEERS, PEERS).astype(jnp.int32)
    parts = [part.astype(F32).astype(BF16) for part in (labels // 32 * 32, labels % 32)]
    ones = jnp.ones((16, PEERS), BF16)

    def prepare(block, carry):
        first = block * BLOCK
        expand = jnp.where((iota((BLOCK, PEERS), 0) + first) // CAP == iota((BLOCK, PEERS), 1), 1.0, 0.0).astype(BF16)
        own_lane = iota((BLOCK, PEERS), 0) % CAP == iota((BLOCK, PEERS), 1)
        spread = [jnp.where(own_lane, dot(expand, part), 0.0) for part in parts]
        column = jnp.sum(spread[0] + spread[1], axis=1, keepdims=True).astype(jnp.int32) - 1
        row = (dot_nt(ones, spread[0].astype(BF16)) + dot_nt(ones, spread[1].astype(BF16)))[0:1].astype(jnp.int32) - 1
        pick = jnp.where(column == iota((BLOCK, ROWS), 1), 1.0, 0.0).astype(BF16)
        pick_recv[block] = dot(pick, recv_proj[...]).astype(BF16)
        pick_node[block] = jnp.where(row == iota((ROWS, BLOCK), 0), 1.0, 0.0).astype(BF16)
        return carry

    lax.fori_loop(0, PEERS * CAP // BLOCK, prepare, 0)

    def arrive(group):
        rows = arriving[pl.ds(group * GROUP, GROUP)].reshape(GROUP * CAP, DIM)
        hidden = swish_half(rows.astype(F32) + pick_recv[group].astype(F32))
        hidden_sum[...] += dot(pick_node[group], hidden)

    def received(group, count):
        block = arriving.at[pl.ds(group * GROUP, count)]
        pltpu.make_async_remote_copy(
            src_ref=block,
            dst_ref=block,
            send_sem=send_sem,
            recv_sem=recv_sem.at[group],
            device_id=(lat, lon),
            device_id_type=MESH,
        ).wait_recv()

    for group in range(GROUPS - 1):
        received(group, GROUP)
        arrive(group)
    own.wait()
    received(GROUPS - 1, GROUP - 1)
    arrive(GROUPS - 1)

    preact = self_part[...] + dot(hidden_sum[...].astype(BF16), fold_enc[...])
    hidden = swish(preact).astype(BF16)
    projected[...] = (receiver[...] + dot(hidden, fold_send[...])).astype(BF16)
    chosen_rows = dot(chooser[...], projected[...]).astype(BF16)
    halo_out[...] = chosen_rows.reshape(PEERS, HALO, DIM)
    for offset in OFFSETS:
        to_lat, to_lon = peer(offset)
        pltpu.make_async_remote_copy(
            src_ref=halo_out.at[to_lat * 16 + to_lon],
            dst_ref=halo_in.at[me],
            send_sem=halo_send_sem,
            recv_sem=halo_recv_sem,
            device_id=(to_lat, to_lon),
            device_id_type=MESH,
        ).start()
    own_halo = pltpu.make_async_copy(halo_out.at[me], halo_in.at[me], own_sem)
    own_halo.start()

    mesh_one[...] = (latent[...].astype(F32) + dot(hidden, weights[ENC_NODE_OUT])).astype(BF16)
    receiver[...] = dot(mesh_one[...], weights[PROC_RECV])

    def gather_local(k, carry):
        local_part[k] = dot(pick_local[k], projected[...]) + receiver[...]
        return carry

    lax.fori_loop(0, DEGREE, gather_local, 0)
    self_part[...] = dot(mesh_one[...], weights[PROC_NODE_SELF])

    own_halo.wait()
    halo_all = halo_in.at[pl.ds(0, PEERS - 1)]
    halo_wait = pltpu.make_async_remote_copy(
        src_ref=halo_all,
        dst_ref=halo_all,
        send_sem=halo_send_sem,
        recv_sem=halo_recv_sem,
        device_id=(lat, lon),
        device_id_type=MESH,
    )
    halo_wait.wait_recv()
    table = halo_in[...].reshape(PEERS * HALO, DIM)
    hidden_sum[...] = jnp.zeros((ROWS, DIM), F32)
    projected[...] = table

    for k in range(DEGREE):
        hidden_sum[...] += swish_half(local_part[k] + dot(pick_halo[k], projected[...])).astype(F32)

    preact = self_part[...] + dot(hidden_sum[...].astype(BF16), fold_proc[...])
    hidden = swish(preact).astype(BF16)
    out_ref[...] = (mesh_one[...].astype(F32) + dot(hidden, weights[PROC_NODE_OUT])).astype(BF16)

    names_wait.wait_send()
    halo_wait.wait_send()
    sent = arriving.at[pl.ds(0, PEERS - 1)]
    pltpu.make_async_remote_copy(
        src_ref=sent,
        dst_ref=sent,
        send_sem=send_sem,
        recv_sem=recv_sem.at[0],
        device_id=(lat, lon),
        device_id_type=MESH,
    ).wait_send()


def on_device(grid_feats, mesh_latent, embed_in, *rest):
    weights = rest[:13]
    dest_dev, dest_node, send_rows, src_slot = rest[13:]
    vmem = pltpu.VMEM
    square = vmem((DIM, DIM), BF16)
    scratch = [
        vmem((CHANNELS, ROWS), BF16),
        vmem((DIM, ROWS), BF16),
        square,
        vmem((CHANNELS, DIM), BF16),
        square,
        vmem((13, DIM, DIM), BF16),
        vmem((2, ROWS), jnp.int32),
        vmem((2, ROWS), jnp.int32),
        vmem((1, HALO, PEERS), jnp.int32),
        vmem((DEGREE, ROWS), jnp.int32),
        vmem((PEERS, CAP, DIM), BF16),
        vmem((PEERS, CAP, DIM), BF16),
        vmem((PEERS, HALO, DIM), BF16),
        vmem((PEERS, HALO, DIM), BF16),
        square,
        vmem((ROWS, DIM), F32),
        square,
        square,
        square,
        square,
        vmem((PEERS, 1, PEERS), F32),
        vmem((PEERS, 1, PEERS), F32),
        vmem((GROUPS, BLOCK, DIM), BF16),
        vmem((GROUPS, ROWS, BLOCK), BF16),
        vmem((ROWS, DIM), F32),
        vmem((PEERS * HALO, ROWS), BF16),
        vmem((DEGREE, ROWS, ROWS), BF16),
        vmem((DEGREE, ROWS, PEERS * HALO), BF16),
        square,
        square,
        vmem((ROWS, DIM), F32),
        vmem((DEGREE, ROWS, DIM), F32),
        pltpu.SemaphoreType.DMA((7,)),
        pltpu.SemaphoreType.DMA((13,)),
        pltpu.SemaphoreType.DMA,
        pltpu.SemaphoreType.DMA((GROUPS,)),
        pltpu.SemaphoreType.DMA,
        pltpu.SemaphoreType.DMA,
        pltpu.SemaphoreType.DMA,
        pltpu.SemaphoreType.DMA((3,)),
    ]
    return pl.pallas_call(
        kernel,
        out_shape=jax.ShapeDtypeStruct((ROWS, DIM), BF16),
        in_specs=[pl.BlockSpec(memory_space=pl.ANY)] * 20,
        out_specs=pl.BlockSpec(memory_space=pltpu.VMEM),
        scratch_shapes=scratch,
        compiler_params=pltpu.CompilerParams(
            collective_id=0, has_side_effects=True, vmem_limit_bytes=56 * 2**20
        ),
    )(
        grid_feats.T,
        mesh_latent,
        embed_in,
        *weights,
        dest_dev.T,
        dest_node.T,
        jnp.swapaxes(send_rows, 1, 2),
        src_slot.T,
    )


def solution(mesh):
    rows = P(("lat", "lon"), None)
    in_specs = (rows, rows, *([P()] * 14), rows, rows, P(("lat", "lon"), None, None), rows)
    return jax.shard_map(on_device, mesh=mesh, in_specs=in_specs, out_specs=rows, check_vma=False)
```

```python
import functools

import jax
import jax.numpy as jnp
from jax import lax
from jax.experimental import pallas as pl
from jax.experimental.pallas import tpu as pltpu
from jax.sharding import PartitionSpec as P

MESH = pl.DeviceIdType.MESH
BF16 = jnp.bfloat16
F32 = jnp.float32
PEERS = 128
CAP = 16
HALO = 4
GROUP = 16
GROUPS = PEERS // GROUP
DIM = 512
CHANNELS = 474
ROWS = 512
TAIL = CHANNELS // 16 * 16
DEGREE = 8
BLOCK = GROUP * CAP

(
    EMBED_OUT,
    ENC_SEND,
    ENC_RECV,
    ENC_EDGE_OUT,
    ENC_NODE_SELF,
    ENC_NODE_AGG,
    ENC_NODE_OUT,
    PROC_SEND,
    PROC_RECV,
    PROC_EDGE_OUT,
    PROC_NODE_SELF,
    PROC_NODE_AGG,
    PROC_NODE_OUT,
) = range(13)


def ring_distance(step):
    return min(step, 4 - step)


OFFSETS = sorted(
    (
        (dy, dc, dx, dz)
        for dy in range(4)
        for dc in range(2)
        for dx in range(4)
        for dz in range(4)
        if (dy, dc, dx, dz) != (0, 0, 0, 0)
    ),
    key=lambda o: -(ring_distance(o[0]) + ring_distance(o[2]) + ring_distance(o[3]) + 0.1 * o[1]),
)


def swish(values):
    return values * (0.5 * jnp.tanh(0.5 * values) + 0.5)


def swish_half(values):
    half = (0.5 * values).astype(BF16)
    return half * jnp.tanh(half) + half


def dot(left, right):
    return jnp.dot(left, right, preferred_element_type=F32)


def dot_nt(left, right):
    return lax.dot_general(left, right, (((1,), (1,)), ((), ())), preferred_element_type=F32)


def dot_tn(left, right):
    return lax.dot_general(left, right, (((0,), (0,)), ((), ())), preferred_element_type=F32)


def iota(shape, dimension):
    return lax.broadcasted_iota(jnp.int32, shape, dimension)


def kernel(
    feats_hbm,
    latent_hbm,
    embed_in_hbm,
    *rest,
):
    weights_hbm = rest[:13]
    (dest_hbm, node_hbm, send_rows_hbm, slot_hbm, out_ref) = rest[13:18]
    (
        feats,
        aug,
        latent,
        embed_raw,
        embed_in,
        weights,
        dest,
        node,
        send_rows,
        slot,
        outgoing,
        arriving,
        halo_out,
        halo_in,
        recv_proj,
        self_part,
        fold_enc,
        fold_proc,
        fold_send,
        sender_part,
        names_out,
        names_in,
        pick_recv,
        pick_node,
        hidden_sum,
        chooser,
        pick_local,
        pick_halo,
        mesh_one,
        projected,
        receiver,
        local_part,
        load_sem,
        weight_sem,
        send_sem,
        recv_sem,
        halo_send_sem,
        halo_recv_sem,
        own_sem,
        names_sem,
    ) = rest[18:]

    lat, lon = lax.axis_index("lat"), lax.axis_index("lon")
    me = lat * 16 + lon
    lats = {(dy, dc): ((lat // 2 + dy) % 4) * 2 + (lat + dc) % 2 for dy in range(4) for dc in range(2)}
    lons = {(dx, dz): ((lon // 4 + dx) % 4) * 4 + (lon + dz) % 4 for dx in range(4) for dz in range(4)}

    def peer(offset):
        dy, dc, dx, dz = offset
        return lats[dy, dc], lons[dx, dz]

    loads = [
        pltpu.make_async_copy(source, target, load_sem.at[i])
        for i, (source, target) in enumerate(
            (
                (dest_hbm, dest),
                (node_hbm, node),
                (feats_hbm, feats),
                (latent_hbm, latent),
                (embed_in_hbm, embed_raw),
                (send_rows_hbm, send_rows),
                (slot_hbm, slot),
            )
        )
    ]
    weight_loads = [
        pltpu.make_async_copy(source, weights.at[i], weight_sem.at[i])
        for i, source in enumerate(weights_hbm)
    ]
    for load in loads[:5]:
        load.start()
    weight_loads[EMBED_OUT].start()
    weight_loads[ENC_SEND].start()

    barrier = pltpu.get_barrier_semaphore()
    for offset in OFFSETS:
        pl.semaphore_signal(barrier, inc=1, device_id=peer(offset), device_id_type=MESH)
    for load in weight_loads[ENC_RECV:] + loads[5:]:
        load.start()

    loads[0].wait()
    loads[1].wait()
    dests = dest[...]
    nodes = node[...]
    owner = iota((PEERS, ROWS), 0)
    hits = [dests[k : k + 1, :] == owner for k in range(2)]
    onehot = [jnp.where(hit, 1.0, 0.0).astype(BF16) for hit in hits]
    earlier = jnp.where(iota((ROWS, ROWS), 0) < iota((ROWS, ROWS), 1), 1.0, 0.0).astype(BF16)
    ranks = dot(jnp.concatenate(onehot, axis=0), earlier)
    first_count = jnp.sum(jnp.where(hits[0], 1.0, 0.0), axis=1, keepdims=True)
    ranks = [
        jnp.sum(jnp.where(hits[0], ranks[:PEERS], 0.0), axis=0, keepdims=True).astype(jnp.int32),
        jnp.sum(jnp.where(hits[1], ranks[PEERS:] + first_count, 0.0), axis=0, keepdims=True).astype(jnp.int32),
    ]
    positions = [dests[k : k + 1] * CAP + ranks[k] for k in range(2)]

    named = jnp.zeros((PEERS, PEERS), F32)
    for k in range(2):
        at_slot = ranks[k] == iota((PEERS, ROWS), 0)
        label = nodes[k : k + 1] + 1
        for part in (label // 32 * 32, label % 32):
            value = jnp.where(at_slot, part.astype(F32), 0.0).astype(BF16)
            named += dot_nt(onehot[k], value)
    names_out[...] = named.reshape(PEERS, 1, PEERS)

    left = CHANNELS - TAIL
    pad = jnp.zeros((16 - left, ROWS), F32)
    rest_pad = jnp.zeros((DIM - TAIL - 16, DIM), BF16)
    for load, raw, padded in ((loads[2], feats, aug), (loads[4], embed_raw, embed_in)):
        load.wait()
        padded[0:TAIL, :] = raw[0:TAIL, :]
        padded[TAIL : TAIL + 16, :] = jnp.concatenate([raw[TAIL:CHANNELS, :].astype(F32), pad], axis=0).astype(BF16)
        padded[TAIL + 16 :, :] = rest_pad
    embedded = swish_half(dot_tn(aug[...], embed_in[...]))
    weight_loads[EMBED_OUT].wait()
    grid_latent = dot(embedded, weights[EMBED_OUT]).astype(BF16)
    weight_loads[ENC_SEND].wait()
    sender_part[...] = dot(grid_latent, weights[ENC_SEND]).astype(BF16)

    def pack(block, carry):
        slots = iota((512, ROWS), 0) + block * 512
        pick = jnp.where((positions[0] == slots) | (positions[1] == slots), 1.0, 0.0).astype(BF16)
        rows = dot(pick, sender_part[...]).astype(BF16)
        outgoing[pl.ds(block * 32, 32)] = rows.reshape(32, CAP, DIM)
        return carry

    lax.fori_loop(0, PEERS * CAP // 512, pack, 0)

    pl.semaphore_wait(barrier, PEERS - 1)
    for step, offset in enumerate(OFFSETS):
        to_lat, to_lon = peer(offset)
        pltpu.make_async_remote_copy(
            src_ref=names_out.at[to_lat * 16 + to_lon],
            dst_ref=names_in.at[step],
            send_sem=names_sem.at[0],
            recv_sem=names_sem.at[1],
            device_id=(to_lat, to_lon),
            device_id_type=MESH,
        ).start()
    own_names = pltpu.make_async_copy(names_out.at[me], names_in.at[PEERS - 1], names_sem.at[2])
    own_names.start()
    for step, offset in enumerate(OFFSETS):
        to_lat, to_lon = peer(offset)
        pltpu.make_async_remote_copy(
            src_ref=outgoing.at[to_lat * 16 + to_lon],
            dst_ref=arriving.at[step],
            send_sem=send_sem,
            recv_sem=recv_sem.at[step // GROUP],
            device_id=(to_lat, to_lon),
            device_id_type=MESH,
        ).start()
    own = pltpu.make_async_copy(outgoing.at[me], arriving.at[PEERS - 1], own_sem)
    own.start()

    loads[3].wait()
    for load in weight_loads[ENC_RECV:]:
        load.wait()
    recv_proj[...] = dot(latent[...], weights[ENC_RECV]).astype(BF16)
    hidden_sum[...] = jnp.zeros((ROWS, DIM), F32)
    self_part[...] = dot(latent[...], weights[ENC_NODE_SELF])
    fold_enc[...] = dot(weights[ENC_EDGE_OUT], weights[ENC_NODE_AGG]).astype(BF16)
    fold_send[...] = dot(weights[ENC_NODE_OUT], weights[PROC_SEND]).astype(BF16)
    receiver[...] = dot(latent[...], weights[PROC_SEND])
    fold_proc[...] = dot(weights[PROC_EDGE_OUT], weights[PROC_NODE_AGG]).astype(BF16)

    loads[5].wait()
    loads[6].wait()
    chosen = send_rows[0]
    chosen = jnp.concatenate([chosen // 32, chosen % 32], axis=0).astype(F32).astype(BF16)
    repeat = jnp.where(iota((PEERS * HALO, PEERS), 0) // HALO == iota((PEERS * HALO, PEERS), 1), 1.0, 0.0)
    chosen = dot_nt(repeat.astype(BF16), chosen)
    column = iota((PEERS * HALO, 2 * HALO), 1)
    chosen = jnp.where(column < HALO, chosen * 32.0, chosen)
    mine = column % HALO == iota((PEERS * HALO, 2 * HALO), 0) % HALO
    chosen = jnp.sum(jnp.where(mine, chosen, 0.0), axis=1, keepdims=True).astype(jnp.int32)
    node_lane = iota((ROWS, ROWS), 1)
    chooser[...] = jnp.where(chosen == node_lane, 1.0, 0.0).astype(BF16)

    slots = slot[...]
    slots = jnp.concatenate([slots // 32, slots % 32], axis=0).astype(F32).astype(BF16)
    identity = jnp.where(iota((ROWS, ROWS), 0) == node_lane, 1.0, 0.0).astype(BF16)
    slots = dot_nt(identity, slots)
    slots = (slots[:, :DEGREE] * 32.0 + slots[:, DEGREE:]).astype(jnp.int32)
    for k in range(DEGREE):
        wanted = slots[:, k : k + 1]
        pick_local[k] = jnp.where(wanted == node_lane, 1.0, 0.0).astype(BF16)
        pick_halo[k] = jnp.where(wanted - ROWS == node_lane, 1.0, 0.0).astype(BF16)

    own_names.wait()
    names_all = names_in.at[pl.ds(0, PEERS - 1)]
    names_wait = pltpu.make_async_remote_copy(
        src_ref=names_all,
        dst_ref=names_all,
        send_sem=names_sem.at[0],
        recv_sem=names_sem.at[1],
        device_id=(lat, lon),
        device_id_type=MESH,
    )
    names_wait.wait_recv()
    labels = names_in[...].reshape(PEERS, PEERS).astype(jnp.int32)
    parts = [part.astype(F32).astype(BF16) for part in (labels // 32 * 32, labels % 32)]
    ones = jnp.ones((16, PEERS), BF16)

    def prepare(block, carry):
        first = block * BLOCK
        expand = jnp.where((iota((BLOCK, PEERS), 0) + first) // CAP == iota((BLOCK, PEERS), 1), 1.0, 0.0).astype(BF16)
        own_lane = iota((BLOCK, PEERS), 0) % CAP == iota((BLOCK, PEERS), 1)
        spread = [jnp.where(own_lane, dot(expand, part), 0.0) for part in parts]
        column = jnp.sum(spread[0] + spread[1], axis=1, keepdims=True).astype(jnp.int32) - 1
        row = (dot_nt(ones, spread[0].astype(BF16)) + dot_nt(ones, spread[1].astype(BF16)))[0:1].astype(jnp.int32) - 1
        pick = jnp.where(column == iota((BLOCK, ROWS), 1), 1.0, 0.0).astype(BF16)
        pick_recv[block] = dot(pick, recv_proj[...]).astype(BF16)
        pick_node[block] = jnp.where(row == iota((ROWS, BLOCK), 0), 1.0, 0.0).astype(BF16)
        return carry

    lax.fori_loop(0, PEERS * CAP // BLOCK, prepare, 0)

    def arrive(group):
        rows = arriving[pl.ds(group * GROUP, GROUP)].reshape(GROUP * CAP, DIM)
        hidden = swish_half(rows.astype(F32) + pick_recv[group].astype(F32))
        hidden_sum[...] += dot(pick_node[group], hidden)

    def received(group, count):
        block = arriving.at[pl.ds(group * GROUP, count)]
        pltpu.make_async_remote_copy(
            src_ref=block,
            dst_ref=block,
            send_sem=send_sem,
            recv_sem=recv_sem.at[group],
            device_id=(lat, lon),
            device_id_type=MESH,
        ).wait_recv()

    for group in range(GROUPS - 1):
        received(group, GROUP)
        arrive(group)
    own.wait()
    received(GROUPS - 1, GROUP - 1)
    arrive(GROUPS - 1)

    preact = self_part[...] + dot(hidden_sum[...].astype(BF16), fold_enc[...])
    hidden = swish_half(preact)
    projected[...] = (receiver[...] + dot(hidden, fold_send[...])).astype(BF16)
    chosen_rows = dot(chooser[...], projected[...]).astype(BF16)
    halo_out[...] = chosen_rows.reshape(PEERS, HALO, DIM)
    for offset in OFFSETS:
        to_lat, to_lon = peer(offset)
        pltpu.make_async_remote_copy(
            src_ref=halo_out.at[to_lat * 16 + to_lon],
            dst_ref=halo_in.at[me],
            send_sem=halo_send_sem,
            recv_sem=halo_recv_sem,
            device_id=(to_lat, to_lon),
            device_id_type=MESH,
        ).start()
    own_halo = pltpu.make_async_copy(halo_out.at[me], halo_in.at[me], own_sem)
    own_halo.start()

    mesh_one[...] = (latent[...].astype(F32) + dot(hidden, weights[ENC_NODE_OUT])).astype(BF16)
    receiver[...] = dot(mesh_one[...], weights[PROC_RECV])

    def gather_local(k, carry):
        local_part[k] = dot(pick_local[k], projected[...]) + receiver[...]
        return carry

    lax.fori_loop(0, DEGREE, gather_local, 0)
    self_part[...] = dot(mesh_one[...], weights[PROC_NODE_SELF])

    own_halo.wait()
    halo_all = halo_in.at[pl.ds(0, PEERS - 1)]
    halo_wait = pltpu.make_async_remote_copy(
        src_ref=halo_all,
        dst_ref=halo_all,
        send_sem=halo_send_sem,
        recv_sem=halo_recv_sem,
        device_id=(lat, lon),
        device_id_type=MESH,
    )
    halo_wait.wait_recv()
    table = halo_in[...].reshape(PEERS * HALO, DIM)
    hidden_sum[...] = jnp.zeros((ROWS, DIM), F32)
    projected[...] = table

    for k in range(DEGREE):
        hidden_sum[...] += swish_half(local_part[k] + dot(pick_halo[k], projected[...])).astype(F32)

    preact = self_part[...] + dot(hidden_sum[...].astype(BF16), fold_proc[...])
    hidden = swish_half(preact)
    out_ref[...] = (mesh_one[...].astype(F32) + dot(hidden, weights[PROC_NODE_OUT])).astype(BF16)

    names_wait.wait_send()
    halo_wait.wait_send()
    sent = arriving.at[pl.ds(0, PEERS - 1)]
    pltpu.make_async_remote_copy(
        src_ref=sent,
        dst_ref=sent,
        send_sem=send_sem,
        recv_sem=recv_sem.at[0],
        device_id=(lat, lon),
        device_id_type=MESH,
    ).wait_send()


def on_device(grid_feats, mesh_latent, embed_in, *rest):
    weights = rest[:13]
    dest_dev, dest_node, send_rows, src_slot = rest[13:]
    vmem = pltpu.VMEM
    square = vmem((DIM, DIM), BF16)
    scratch = [
        vmem((CHANNELS, ROWS), BF16),
        vmem((DIM, ROWS), BF16),
        square,
        vmem((CHANNELS, DIM), BF16),
        square,
        vmem((13, DIM, DIM), BF16),
        vmem((2, ROWS), jnp.int32),
        vmem((2, ROWS), jnp.int32),
        vmem((1, HALO, PEERS), jnp.int32),
        vmem((DEGREE, ROWS), jnp.int32),
        vmem((PEERS, CAP, DIM), BF16),
        vmem((PEERS, CAP, DIM), BF16),
        vmem((PEERS, HALO, DIM), BF16),
        vmem((PEERS, HALO, DIM), BF16),
        square,
        vmem((ROWS, DIM), F32),
        square,
        square,
        square,
        square,
        vmem((PEERS, 1, PEERS), F32),
        vmem((PEERS, 1, PEERS), F32),
        vmem((GROUPS, BLOCK, DIM), BF16),
        vmem((GROUPS, ROWS, BLOCK), BF16),
        vmem((ROWS, DIM), F32),
        vmem((PEERS * HALO, ROWS), BF16),
        vmem((DEGREE, ROWS, ROWS), BF16),
        vmem((DEGREE, ROWS, PEERS * HALO), BF16),
        square,
        square,
        vmem((ROWS, DIM), F32),
        vmem((DEGREE, ROWS, DIM), F32),
        pltpu.SemaphoreType.DMA((7,)),
        pltpu.SemaphoreType.DMA((13,)),
        pltpu.SemaphoreType.DMA,
        pltpu.SemaphoreType.DMA((GROUPS,)),
        pltpu.SemaphoreType.DMA,
        pltpu.SemaphoreType.DMA,
        pltpu.SemaphoreType.DMA,
        pltpu.SemaphoreType.DMA((3,)),
    ]
    return pl.pallas_call(
        kernel,
        out_shape=jax.ShapeDtypeStruct((ROWS, DIM), BF16),
        in_specs=[pl.BlockSpec(memory_space=pl.ANY)] * 20,
        out_specs=pl.BlockSpec(memory_space=pltpu.VMEM),
        scratch_shapes=scratch,
        compiler_params=pltpu.CompilerParams(
            collective_id=0, has_side_effects=True, vmem_limit_bytes=56 * 2**20
        ),
    )(
        grid_feats.T,
        mesh_latent,
        embed_in,
        *weights,
        dest_dev.T,
        dest_node.T,
        jnp.swapaxes(send_rows, 1, 2),
        src_slot.T,
    )


def solution(mesh):
    rows = P(("lat", "lon"), None)
    in_specs = (rows, rows, *([P()] * 14), rows, rows, P(("lat", "lon"), None, None), rows)
    return jax.shard_map(on_device, mesh=mesh, in_specs=in_specs, out_specs=rows, check_vma=False)
```
